256 devices in a mesh: span: 4 (over x_lo, core), plane: 64 (over y, x_hi, z).
Axes of the slice: x: 4 (x_hi: 2, x_lo: 2; x = x_hi * 2 + x_lo), y: 4, z: 8, core: 2. Of those that a mesh axis runs over, the one named last changes fastest.
Arguments:
- snapshot: float32 [262144, 512], P('plane', 'span')
- factor: float32 [512, 64], P('span'), may hold values from -0.25 to 0.25
Outputs:
- gram: float32 [512, 512], P('span')
- core: float32 [64, 262144], P(None, ('plane', 'span'))
The draws below stay inside these ranges and needn't reach their ends.
All inputs are finite; a program needn't handle non-finite values.
Results may differ from the reference program's by a relative error of at most 0.000073.
Values sent between devices are 32-bit elements; how exact they have to be, the bound alone decides.
A program may use at most 64 MiB of HBM per device.

```python
import math
import jax
import jax.numpy as jnp
from jax import lax

SPAN = 512
RANK = 64
FIBRES = 262144


def draw_snapshot(key, part):
    key = jax.random.fold_in(key, 7)
    key_row, key_col, key_base, key_shift, key_mix = jax.random.split(key, 5)
    position = jnp.arange(FIBRES, dtype=jnp.float32) / FIBRES
    row_scale = jnp.exp(math.log(10.0) * position)[:, None] * jax.random.uniform(key_row, (FIBRES, 1), jnp.float32, 0.6, 1.6)
    col_scale = jnp.exp(jax.random.uniform(key_col, (1, SPAN), jnp.float32, 0.0, math.log(4.0)))
    noise_field = jnp.clip(jax.random.normal(key_base, (FIBRES, SPAN), jnp.float32), -5.0, 5.0)
    shifts = jax.random.randint(key_shift, (8,), 1, SPAN)
    mixing = jax.random.uniform(key_mix, (8, SPAN), jnp.float32, -0.7, 0.7)
    spanwise = jnp.arange(SPAN, dtype=jnp.int32)
    correlated = noise_field
    for shift_index in range(8):
        source = (spanwise - shifts[shift_index]) % SPAN
        shifted = jnp.take(noise_field, source, axis=1)
        correlated = correlated + mixing[shift_index][None, :] * shifted
    return row_scale * col_scale * correlated


def shard_levels(rng, shape, cuts, low, high):
    def one(axis_at, shards_of):
        steps = jax.random.uniform(jax.random.fold_in(jax.random.fold_in(rng, 6), axis_at), (shards_of,), jnp.float32, low / len(cuts), high / len(cuts))
        return jnp.repeat(jnp.exp(steps), shape[axis_at] // shards_of).reshape((-1,) + (1,) * (len(shape) - axis_at - 1))

    level = one(*cuts[0])
    for cut in cuts[1:]:
        level = level * one(*cut)
    return level


def normal_values(key, dims, spread, most, pieces=(), held_as=jnp.bfloat16):
    gain = shard_levels(key, dims, pieces, -0.22, 0.18) if pieces else 1.0
    entries = jax.random.normal(key, dims, jnp.float32) * spread * gain
    return jnp.minimum(jnp.maximum(entries, -most), most).astype(held_as)


def setup_inputs(seed: int = 0) -> dict:
    arg_keys = jax.random.split(jax.random.key(seed), 3)
    return {
        "snapshot": draw_snapshot(jax.random.fold_in(arg_keys[2], 71), 0),
        "factor": normal_values(arg_keys[1], (SPAN, RANK), SPAN ** -0.5, 0.25, ((0, 4),), jnp.float32),
    }


def reference(snapshot, factor):
    gram = jnp.dot(snapshot.T, snapshot, preferred_element_type=jnp.float32, precision=lax.Precision.HIGHEST) / FIBRES
    core = jnp.dot(factor.T, snapshot.T, preferred_element_type=jnp.float32, precision=lax.Precision.HIGHEST)
    return gram, core
```

```python
import functools

import jax
import jax.numpy as jnp
from jax import lax
from jax.experimental import pallas as pl
from jax.experimental.pallas import tpu as pltpu
from jax.sharding import PartitionSpec as P

MESH = pl.DeviceIdType.MESH
F32, BF16 = jnp.float32, jnp.bfloat16

ROWS, COLS, RANK = 4096, 128, 64
HALF = ROWS // 2
PART = ROWS // 4
NC, CH = 4, 32
NU, NZ = 8, 8
BLK = 512


def split(v):
    hi = v.astype(BF16)
    return hi, (v - hi.astype(F32)).astype(BF16)


def dot(a, b):
    return jnp.dot(a, b, preferred_element_type=F32)


def dot3(a, b_hi, b_lo):
    m = a.shape[0]
    a_hi, a_lo = split(a)
    both = dot(jnp.concatenate([a_hi, a_lo], 0), b_hi)
    return both[:m] + both[m:] + dot(a_hi, b_lo)


def kernel(
    scale, x_hbm, f_ref, gram_ref, core_ref,
    nat, pnat, st, xt, ft, abh, abl, eacc,
    rt, p1, zb, wb, rp, qb, et, ep1, ez, eb, tt, tr,
    ld, cs, cr, fs, fr, xs, xr, s1, r1, s2, r2, s3, r3, s4, r4, ts, trs,
):
    s, p = lax.axis_index("span"), lax.axis_index("plane")
    l, c = s // 2, s % 2
    u, z = p // NZ, p % NZ
    h, g = u // 4, u % 4

    def dev(l, c, u, z):
        return {"span": l * 2 + c, "plane": u * NZ + z}

    def ahead(k):
        return lax.rem(u + k, NU)

    def remote(src, dst, send, recv, to):
        return pltpu.make_async_remote_copy(
            src_ref=src, dst_ref=dst, send_sem=send, recv_sem=recv, device_id=to, device_id_type=MESH
        )

    def wait_bytes(ref, sem):
        pltpu.make_async_copy(ref, ref, sem).wait()

    barrier = pltpu.get_barrier_semaphore()
    for k in range(NU):
        uu = ahead(k)
        pl.semaphore_signal(barrier, inc=1, device_id=dev(1 - l, c, uu, z), device_id_type=MESH)
        pl.semaphore_signal(barrier, inc=1, device_id=dev(l, 1 - c, uu, z), device_id_type=MESH)
        if k:
            pl.semaphore_signal(barrier, inc=1, device_id=dev(l, c, uu, z), device_id_type=MESH)
    for k in range(1, NZ):
        pl.semaphore_signal(barrier, inc=1, device_id=dev(l, c, u, lax.rem(z + k, NZ)), device_id_type=MESH)

    here = [pl.ds(pl.multiple_of((1 - l) * HALF, HALF), HALF), pl.ds(pl.multiple_of(l * HALF, HALF), HALF)]
    loads = [pltpu.make_async_copy(x_hbm.at[here[i]], nat.at[i], ld.at[i]) for i in range(2)]
    loads[0].start()
    loads[1].start()
    ft[0] = f_ref[...]

    def turn(i):
        def step(b, _):
            at = pl.ds(pl.multiple_of(b * 128, 128), 128)
            st[i, :, at] = nat[i, at, :].T
            return 0

        lax.fori_loop(0, HALF // 128, step, 0, unroll=4)

    loads[0].wait()
    turn(0)
    pl.semaphore_wait(barrier, 3 * NU - 1 + NZ - 1)

    xpeer, cpeer = dev(1 - l, c, u, z), dev(l, 1 - c, u, z)
    chunk = [pl.ds(k * CH, CH) for k in range(NC)]
    xcopy = [remote(st.at[0, chunk[k]], xt.at[chunk[k]], xs.at[k], xr.at[k], xpeer) for k in range(NC)]
    ccopy = [remote(x_hbm.at[here[i]], pnat.at[i], cs.at[i], cr.at[i], cpeer) for i in range(2)]
    fcopy = remote(ft.at[0], ft.at[1], fs, fr, xpeer)
    ccopy[1].start()
    xcopy[0].start()
    fcopy.start()
    for k in range(1, NC):
        xcopy[k].start()
    ccopy[0].start()
    loads[1].wait()
    turn(1)

    def inchip(i, keep):
        def step(b, _):
            at = pl.ds(pl.multiple_of(b * BLK, BLK), BLK)
            ab_hi, ab_lo = split(jnp.concatenate([nat[i, at, :], pnat[i, at, :]], 1))
            if keep:
                abh[at, :] = ab_hi
                abl[at, :] = ab_lo
            eacc[...] += dot3(st[i, :, at], ab_hi, ab_lo)
            return 0

        lax.fori_loop(0, HALF // BLK, step, 0)

    eacc[...] = jnp.zeros_like(eacc)
    ccopy[1].wait_recv()
    inchip(1, True)
    ccopy[0].wait_recv()
    inchip(0, False)

    def tiles(v, k, put):
        for q in range(CH // 8):
            put(c * 4 + q, k, v[q * 8 : q * 8 + 8, :128])
            put((1 - c) * 4 + q, k, v[q * 8 : q * 8 + 8, 128:])

    def put_e(t, k, v):
        et[t, k] = v

    def put_r(t, k, v):
        rt[k, t] = v

    for k in range(NC):
        tiles(eacc[chunk[k], :], k, put_e)
    for k in range(1, NU):
        remote(et.at[ahead(k)], ep1.at[k - 1], s1.at[NC], r1.at[NC], dev(l, c, ahead(k), z)).start()

    def stage1(k):
        xcopy[k].wait_recv()
        tiles(dot3(xt[chunk[k], :], abh[...], abl[...]), k, put_r)
        for j in range(1, NU):
            remote(rt.at[k, ahead(j)], p1.at[k, j - 1], s1.at[k], r1.at[k], dev(l, c, ahead(j), z)).start()

    def stage2(k):
        wait_bytes(p1.at[k], r1.at[k])
        total = rt[k, u]
        for j in range(NU - 1):
            total += p1[k, j]
        zb[k, z] = total
        for j in range(1, NZ):
            remote(zb.at[k, z], zb.at[k, z], s2.at[k], r2.at[k], dev(l, c, u, lax.rem(z + j, NZ))).start()

    def stage3(k):
        wait_bytes(zb.at[k, pl.ds(0, NZ - 1)], r2.at[k])
        total = zb[k, 0]
        for j in range(1, NZ):
            total += zb[k, j]
        wb[k] = total
        for j in range(NU):
            remote(wb.at[k], rp.at[k, u], s3.at[k], r3.at[k], dev(1 - l, c, ahead(j), z)).start()
        for j in range(1, NU):
            remote(wb.at[k], qb.at[c, k, g], s4.at[k], r4.at[k], dev(l, h, ahead(j), z)).start()

        @pl.when(h == c)
        def _():
            pltpu.make_async_copy(wb.at[k], qb.at[c, k, g], r4.at[k]).start()

        @pl.when(h != c)
        def _():
            remote(wb.at[k], qb.at[c, k, g], s4.at[k], r4.at[k], dev(l, h, u, z)).start()

    def estage2():
        wait_bytes(ep1, r1.at[NC])
        total = et[u]
        for j in range(NU - 1):
            total += ep1[j]
        ez[z] = total
        for j in range(1, NZ):
            remote(ez.at[z], ez.at[z], s2.at[NC], r2.at[NC], dev(l, c, u, lax.rem(z + j, NZ))).start()

    def estage3():
        wait_bytes(ez.at[pl.ds(0, NZ - 1)], r2.at[NC])
        total = ez[0]
        for j in range(1, NZ):
            total += ez[j]
        eb[u] = total
        for j in range(1, NU):
            remote(eb.at[u], eb.at[u], s3.at[NC], r3.at[NC], dev(l, c, ahead(j), z)).start()

    stage1(0)
    estage2()
    stage1(1)
    stage2(0)
    estage3()
    stage1(2)
    stage2(1)
    stage3(0)
    stage1(3)
    stage2(2)
    stage3(1)

    fcopy.wait_recv()
    f_hi, f_lo = split(jnp.concatenate([ft[0], ft[1]], 1))
    for j in range(2):
        for b in range(PART // 256):
            at = pl.ds(j * PART + b * 256, 256)
            v_hi, v_lo = split(jnp.concatenate([st[1, :, at], xt[:, at]], 0))
            both = dot(jnp.concatenate([f_hi, f_lo], 0), v_hi)
            tt[j, :, pl.ds(b * 256, 256)] = both[:RANK] + both[RANK:] + dot(f_hi, v_lo)
    tcopy = remote(tt.at[1 - c], tr, ts, trs, cpeer)
    tcopy.start()

    stage2(3)
    stage3(2)

    tcopy.wait_recv()
    core_ref[...] = tt[c] + tr[...]
    inner = [pl.multiple_of(l * 256 + q * 128, 128) for q in range(2)]
    outer = [pl.multiple_of((1 - l) * 256 + q * 128, 128) for q in range(2)]
    wait_bytes(eb.at[pl.ds(0, NU - 1)], r3.at[NC])
    for t in range(NU):
        for k in range(NC):
            gram_ref[pl.ds(k * CH + (t % 4) * 8, 8), pl.ds(inner[t // 4], 128)] = eb[t, k] * scale

    stage3(3)
    for k in range(NC):
        wait_bytes(rp.at[k], r3.at[k])
        wait_bytes(rp.at[k], r4.at[k])
    for q in range(2):
        direct = jnp.concatenate([rp[k, q * 4 + j] for k in range(NC) for j in range(4)], 0)
        turned = qb[q].reshape(COLS, COLS).T
        gram_ref[:, pl.ds(outer[q], 128)] = (direct + turned) * scale

    for i in range(2):
        ccopy[i].wait_send()
    fcopy.wait_send()
    tcopy.wait_send()
    for k in range(NC):
        xcopy[k].wait_send()
        wait_bytes(p1.at[k], s1.at[k])
        wait_bytes(zb.at[k, pl.ds(0, NZ - 1)], s2.at[k])
        wait_bytes(rp.at[k], s3.at[k])

        @pl.when(h == c)
        def _():
            wait_bytes(rp.at[k, pl.ds(0, NU - 1)], s4.at[k])

        @pl.when(h != c)
        def _():
            wait_bytes(rp.at[k], s4.at[k])

    wait_bytes(ep1, s1.at[NC])
    wait_bytes(ez.at[pl.ds(0, NZ - 1)], s2.at[NC])
    wait_bytes(eb.at[pl.ds(0, NU - 1)], s3.at[NC])


def local(snapshot, factor):
    fibres = snapshot.shape[0] * lax.axis_size("plane")
    dma = pltpu.SemaphoreType.DMA
    tile = (8, 128)
    return pl.pallas_call(
        functools.partial(kernel, 1.0 / fibres),
        out_shape=[
            jax.ShapeDtypeStruct((COLS, 4 * COLS), F32),
            jax.ShapeDtypeStruct((RANK, PART), F32),
        ],
        in_specs=[pl.BlockSpec(memory_space=pl.ANY), pl.BlockSpec(memory_space=pltpu.VMEM)],
        out_specs=[pl.BlockSpec(memory_space=pltpu.VMEM)] * 2,
        scratch_shapes=[
            pltpu.VMEM((2, HALF, COLS), F32),
            pltpu.VMEM((2, HALF, COLS), F32),
            pltpu.VMEM((2, COLS, HALF), F32),
            pltpu.VMEM((COLS, HALF), F32),
            pltpu.VMEM((2, RANK, COLS), F32),
            pltpu.VMEM((HALF, 2 * COLS), BF16),
            pltpu.VMEM((HALF, 2 * COLS), BF16),
            pltpu.VMEM((COLS, 2 * COLS), F32),
            pltpu.VMEM((NC, NU) + tile, F32),
            pltpu.VMEM((NC, NU - 1) + tile, F32),
            pltpu.VMEM((NC, NZ) + tile, F32),
            pltpu.VMEM((NC,) + tile, F32),
            pltpu.VMEM((NC, NU) + tile, F32),
            pltpu.VMEM((2, NC, 4) + tile, F32),
            pltpu.VMEM((NU, NC) + tile, F32),
            pltpu.VMEM((NU - 1, NC) + tile, F32),
            pltpu.VMEM((NZ, NC) + tile, F32),
            pltpu.VMEM((NU, NC) + tile, F32),
            pltpu.VMEM((2, RANK, PART), F32),
            pltpu.VMEM((RANK, PART), F32),
            dma((2,)), dma((2,)), dma((2,)), dma, dma, dma((NC,)), dma((NC,)),
            dma((NC + 1,)), dma((NC + 1,)), dma((NC + 1,)), dma((NC + 1,)),
            dma((NC + 1,)), dma((NC + 1,)), dma((NC,)), dma((NC,)), dma, dma,
        ],
        compiler_params=pltpu.CompilerParams(
            collective_id=0, has_side_effects=True, vmem_limit_bytes=56 * 2**20
        ),
    )(snapshot, factor.T)


def solution(mesh):
    return jax.shard_map(
        local,
        mesh=mesh,
        in_specs=(P("plane", "span"), P("span", None)),
        out_specs=(P("span", None), P(None, ("plane", "span"))),
        check_vma=False,
    )
```

```python
import functools

import jax
import jax.numpy as jnp
from jax import lax
from jax.experimental import pallas as pl
from jax.experimental.pallas import tpu as pltpu
from jax.sharding import PartitionSpec as P

MESH = pl.DeviceIdType.MESH
F32, BF16 = jnp.float32, jnp.bfloat16

ROWS, COLS, RANK = 4096, 128, 64
HALF = ROWS // 2
PART = ROWS // 4
NY, NX, NZ = 4, 2, 8
BIG = (48, 32, 32)
SMALL = (8, 8)
SIZES = BIG + SMALL
NB, NS, NC = len(BIG), len(SMALL), len(SIZES)
FIRST = tuple(sum(SIZES[:k]) for k in range(NC))
BLK = 512


def split(v):
    hi = v.astype(BF16)
    return hi, (v - hi.astype(F32)).astype(BF16)


def dot(a, b):
    return jnp.dot(a, b, preferred_element_type=F32)


def dot3(a, b_hi, b_lo):
    m = a.shape[0]
    hi = a.astype(BF16).astype(F32)
    both = dot(jnp.concatenate([hi, a - hi], 0).astype(BF16), b_hi)
    return both[:m] + both[m:] + dot(hi.astype(BF16), b_lo)


def kernel(scale, x_hbm, f_ref, gram_ref, core_ref, *scratch):
    scratch = list(scratch)

    def take(n=None):
        if n is None:
            return scratch.pop(0)
        return [scratch.pop(0) for _ in range(n)]

    nat, pnat, st, xt, ft, abh, abl, eacc, tt, tr = take(10)
    rt, p1, zb = take(NB + 1), take(NB + 1), take(NB + 1)
    wb, rp, qb = take(NB), take(NB), take(NB)
    eb = take()
    z2, w2, rp2, qb2 = take(NS), take(NS), take(NS), take(NS)
    ld, cs, cr, fs, fr, xs, xr, s1, r1, s2, r2, s3, r3, s4, r4, ts, trs = take(17)

    s, p = lax.axis_index("span"), lax.axis_index("plane")
    l, c = s // 2, s % 2
    z = p % NZ
    x = (p // NZ) % NX
    y = p // (NZ * NX)
    h, v = y // 2, y % 2

    def dev(l, c, y, x, z):
        return {"span": l * 2 + c, "plane": (y * NX + x) * NZ + z}

    def yy(k):
        return lax.rem(y + k, NY)

    def zz(k):
        return lax.rem(z + k, NZ)

    def place(k):
        return yy(k + 1), lax.rem(x + 1 + k // NY, NX)

    def each(first, last, do):
        def step(k, _):
            do(k)
            return 0

        lax.fori_loop(first, last, step, 0)

    here_last = NX * NY - 1
    w = x * NY + y

    def remote(src, dst, send, recv, to):
        return pltpu.make_async_remote_copy(
            src_ref=src, dst_ref=dst, send_sem=send, recv_sem=recv, device_id=to, device_id_type=MESH
        )

    def wait_bytes(ref, sem):
        pltpu.make_async_copy(ref, ref, sem).wait()

    barrier = pltpu.get_barrier_semaphore()

    def greet(*to):
        pl.semaphore_signal(barrier, inc=1, device_id=dev(*to), device_id_type=MESH)

    def greet_places(k):
        greet(1 - l, c, *place(k), z)
        greet(l, 1 - c, *place(k), z)

    each(0, NX * NY, greet_places)
    each(0, here_last, lambda k: greet(l, c, *place(k), z))
    each(1, NZ, lambda k: greet(l, c, y, x, zz(k)))

    here = [pl.ds(pl.multiple_of((1 - l) * HALF, HALF), HALF), pl.ds(pl.multiple_of(l * HALF, HALF), HALF)]
    loads = [pltpu.make_async_copy(x_hbm.at[here[i]], nat.at[i], ld.at[i]) for i in range(2)]
    loads[0].start()
    loads[1].start()
    ft[0] = f_ref[...]

    def turn(i):
        def step(b, _):
            at = pl.ds(pl.multiple_of(b * 128, 128), 128)
            st[i, :, at] = nat[i, at, :].T
            return 0

        lax.fori_loop(0, HALF // 128, step, 0, unroll=2)

    loads[0].wait()
    turn(0)
    pl.semaphore_wait(barrier, 3 * NY * NX - 1 + NZ - 1)

    xpeer, cpeer = dev(1 - l, c, y, x, z), dev(l, 1 - c, y, x, z)
    chunk = [pl.ds(FIRST[k], SIZES[k]) for k in range(NC)]
    xcopy = [remote(st.at[0, chunk[k]], xt.at[chunk[k]], xs.at[k], xr.at[k], xpeer) for k in range(NC)]
    ccopy = [remote(x_hbm.at[here[i]], pnat.at[i], cs.at[i], cr.at[i], cpeer) for i in range(2)]
    fcopy = remote(ft.at[0], ft.at[1], fs, fr, xpeer)
    xcopy[0].start()
    ccopy[1].start()
    for k in range(1, NC):
        xcopy[k].start()
    ccopy[0].start()
    fcopy.start()
    loads[1].wait()
    turn(1)

    def inchip(i, keep):
        def step(b, _):
            at = pl.ds(pl.multiple_of(b * BLK, BLK), BLK)
            ab_hi, ab_lo = split(jnp.concatenate([nat[i, at, :], pnat[i, at, :]], 1))
            if keep:
                abh[at, :] = ab_hi
                abl[at, :] = ab_lo
            eacc[...] += dot3(st[i, :, at], ab_hi, ab_lo)
            return 0

        lax.fori_loop(0, HALF // BLK, step, 0)

    def scatter(k, slab):
        n = slab.shape[0] // 2
        for half in range(2):
            rt[k][c * 2 + half] = slab[half * n : half * n + n, :128]
            rt[k][(1 - c) * 2 + half] = slab[half * n : half * n + n, 128:]
        for j in (2, 1, 3):
            remote(rt[k].at[yy(j)], p1[k].at[j - 1], s1.at[k], r1.at[k], dev(l, c, yy(j), x, z)).start()

    def sum_y(k):
        wait_bytes(p1[k], r1.at[k])
        zb[k][z] = rt[k][y] + p1[k][0] + p1[k][1] + p1[k][2]
        each(1, NZ, lambda j: remote(zb[k].at[z], zb[k].at[z], s2.at[k], r2.at[k], dev(l, c, y, x, zz(j))).start())

    def sum_z(ref, k):
        wait_bytes(ref.at[pl.ds(0, NZ - 1)], r2.at[k])
        total = ref[0]
        for j in range(1, NZ):
            total += ref[j]
        return total

    def gather(k):
        wb[k][...] = sum_z(zb[k], k)
        mine = qb[k].at[c, x * 2 + v]
        each(0, NX * NY, lambda o: remote(wb[k], rp[k].at[w], s3.at[k], r3.at[k], dev(1 - l, c, *place(o), z)).start())
        each(0, here_last, lambda o: remote(wb[k], mine, s4.at[k], r4.at[k], dev(l, h, *place(o), z)).start())

        @pl.when(h == c)
        def _():
            pltpu.make_async_copy(wb[k], mine, r4.at[k]).start()

        @pl.when(h != c)
        def _():
            remote(wb[k], mine, s4.at[k], r4.at[k], dev(l, h, y, x, z)).start()

    def gather_inchip():
        eb[w] = sum_z(zb[NB], NB)
        each(0, here_last, lambda o: remote(eb.at[w], eb.at[w], s3.at[NC], r3.at[NC], dev(l, c, *place(o), z)).start())

    def slab_of(k):
        xcopy[k].wait_recv()

        def step(b, total):
            at = pl.ds(pl.multiple_of(b * BLK, BLK), BLK)
            return total + dot3(xt[chunk[k], at], abh[at, :], abl[at, :])

        return lax.fori_loop(0, HALF // BLK, step, jnp.zeros((SIZES[k], 2 * COLS), F32))

    def spread_z(i):
        k = NB + i
        slab = slab_of(k)
        z2[i][z, c] = slab[:, :128]
        z2[i][z, 1 - c] = slab[:, 128:]
        each(1, NZ, lambda j: remote(z2[i].at[z], z2[i].at[z], s2.at[k + 1], r2.at[k + 1], dev(l, c, y, x, zz(j))).start())

    def spread_xy(i):
        k = NB + i
        w2[i][...] = sum_z(z2[i], k + 1)
        mine = qb2[i].at[c * NX * NY + w]

        def send(o):
            to = place(o)
            remote(w2[i], rp2[i].at[w], s3.at[k], r3.at[k], dev(1 - l, c, *to, z)).start()
            remote(w2[i].at[1 - c], mine, s4.at[k], r4.at[k], dev(l, 1 - c, *to, z)).start()

        each(0, NX * NY, send)
        each(0, here_last, lambda o: remote(w2[i].at[c], mine, s4.at[k], r4.at[k], dev(l, c, *place(o), z)).start())
        pltpu.make_async_copy(w2[i].at[c], mine, r4.at[k]).start()

    eacc[...] = jnp.zeros_like(eacc)
    ccopy[1].wait_recv()
    inchip(1, True)
    ccopy[0].wait_recv()
    inchip(0, False)
    scatter(NB, eacc[...])
    scatter(0, slab_of(0))
    sum_y(NB)
    sum_y(0)
    scatter(1, slab_of(1))
    gather_inchip()
    sum_y(1)
    gather(0)
    scatter(2, slab_of(2))
    spread_z(0)
    spread_z(1)
    sum_y(2)
    gather(1)

    fcopy.wait_recv()
    f_hi, f_lo = split(jnp.concatenate([ft[0], ft[1]], 1))
    f_both = jnp.concatenate([f_hi, f_lo], 0)

    def project(b, _):
        at = pl.ds(pl.multiple_of(b * 256, 256), 256)
        v_hi, v_lo = split(jnp.concatenate([st[1, :, at], xt[:, at]], 0))
        both = dot(f_both, v_hi)
        to = pl.ds(pl.multiple_of(b % 4 * 256, 256), 256)
        tt[b // 4, :, to] = both[:RANK] + both[RANK:] + dot(f_hi, v_lo)
        return 0

    lax.fori_loop(0, HALF // 256, project, 0)
    tcopy = remote(tt.at[1 - c], tr, ts, trs, cpeer)
    tcopy.start()

    spread_xy(0)
    spread_xy(1)
    gather(2)

    tcopy.wait_recv()
    core_ref[...] = tt[c] + tr[...]
    wait_bytes(eb.at[pl.ds(0, here_last)], r3.at[NC])
    for q in range(2):
        at = pl.ds(pl.multiple_of(l * 256 + q * 128, 128), 128)
        gram_ref[:, at] = jnp.concatenate([(eb[q * 2 + i] + eb[NY + q * 2 + i]) * scale for i in range(2)], 0)

    for k in range(NC):
        for r, m in ((rp, rp2), (qb, qb2)):
            sem = (r3 if r is rp else r4).at[k]
            wait_bytes(r[k] if k < NB else m[k - NB], sem)

    def all_places(pieces):
        total = pieces[0]
        for piece in pieces[1:]:
            total += piece
        return total

    for q in range(2):
        direct, turned = [], []
        for k in range(NB):
            for i in range(2):
                direct.append(rp[k][q * 2 + i] + rp[k][NY + q * 2 + i])
                turned.append(qb[k][q, i] + qb[k][q, 2 + i])
        for i in range(NS):
            direct.append(all_places([rp2[i][j, q] for j in range(NX * NY)]))
            turned.append(all_places([qb2[i][q * NX * NY + j] for j in range(NX * NY)]))
        at = pl.ds(pl.multiple_of((1 - l) * 256 + q * 128, 128), 128)
        gram_ref[:, at] = (jnp.concatenate(direct, 0) + jnp.concatenate(turned, 0).T) * scale

    for i in range(2):
        ccopy[i].wait_send()
    fcopy.wait_send()
    tcopy.wait_send()
    for k in range(NC):
        xcopy[k].wait_send()
    for k in range(NB + 1):
        wait_bytes(p1[k], s1.at[k])
        wait_bytes(zb[k].at[pl.ds(0, NZ - 1)], s2.at[k])
    for k in range(NB):
        wait_bytes(rp[k], s3.at[k])

        @pl.when(h == c)
        def _():
            wait_bytes(rp[k].at[pl.ds(0, here_last)], s4.at[k])

        @pl.when(h != c)
        def _():
            wait_bytes(rp[k], s4.at[k])

    wait_bytes(eb.at[pl.ds(0, here_last)], s3.at[NC])
    for i in range(NS):
        k = NB + i
        wait_bytes(z2[i].at[pl.ds(0, NZ - 1)], s2.at[k + 1])
        wait_bytes(rp2[i], s3.at[k])
        wait_bytes(qb2[i].at[pl.ds(0, 2 * NX * NY - 1)], s4.at[k])


def write(gram_ref, core_ref, gram_out, core_out):
    gram_out[...] = gram_ref[...]
    core_out[...] = core_ref[...]


def local(snapshot, factor):
    fibres = snapshot.shape[0] * lax.axis_size("plane")
    dma = pltpu.SemaphoreType.DMA

    def vmem(*shape, dtype=F32):
        return pltpu.VMEM(shape, dtype)

    pieces = [n // 2 for n in BIG]
    with_e = pieces + [COLS // 2]
    outs = [((COLS, 4 * COLS), F32), ((RANK, PART), F32)]
    made = pl.pallas_call(
        functools.partial(kernel, 1.0 / fibres),
        out_shape=[jax.ShapeDtypeStruct(*o) for o in outs],
        in_specs=[pl.BlockSpec(memory_space=pl.ANY), pl.BlockSpec(memory_space=pltpu.VMEM)],
        out_specs=[pl.BlockSpec(memory_space=pltpu.VMEM)] * 2,
        scratch_shapes=[
            vmem(2, HALF, COLS),
            vmem(2, HALF, COLS),
            vmem(2, COLS, HALF),
            vmem(COLS, HALF),
            vmem(2, RANK, COLS),
            vmem(HALF, 2 * COLS, dtype=BF16),
            vmem(HALF, 2 * COLS, dtype=BF16),
            vmem(COLS, 2 * COLS),
            vmem(2, RANK, PART),
            vmem(RANK, PART),
        ]
        + [vmem(NY, n, 128) for n in with_e]
        + [vmem(NY - 1, n, 128) for n in with_e]
        + [vmem(NZ, n, 128) for n in with_e]
        + [vmem(n, 128) for n in pieces]
        + [vmem(NX * NY, n, 128) for n in pieces]
        + [vmem(2, NX * 2, n, 128) for n in pieces]
        + [vmem(NX * NY, COLS // 2, 128)]
        + [vmem(NZ, 2, n, 128) for n in SMALL]
        + [vmem(2, n, 128) for n in SMALL]
        + [vmem(NX * NY, 2, n, 128) for n in SMALL]
        + [vmem(2 * NX * NY, n, 128) for n in SMALL]
        + [dma((2,)), dma((2,)), dma((2,)), dma, dma, dma((NC,)), dma((NC,))]
        + [dma((NB + 1,)), dma((NB + 1,)), dma((NC + 1,)), dma((NC + 1,))]
        + [dma((NC + 1,)), dma((NC + 1,)), dma((NC,)), dma((NC,)), dma, dma],
        compiler_params=pltpu.CompilerParams(
            collective_id=0, has_side_effects=True, vmem_limit_bytes=60 * 2**20
        ),
    )(snapshot, factor.T)
    return pl.pallas_call(
        write,
        out_shape=[jax.ShapeDtypeStruct(*o) for o in outs],
    )(*made)


def solution(mesh):
    return jax.shard_map(
        local,
        mesh=mesh,
        in_specs=(P("plane", "span"), P("span", None)),
        out_specs=(P("span", None), P(None, ("plane", "span"))),
        check_vma=False,
    )
```

```python
import functools

import jax
import jax.numpy as jnp
from jax import lax
from jax.experimental import pallas as pl
from jax.experimental.pallas import tpu as pltpu
from jax.sharding import PartitionSpec as P

MESH = pl.DeviceIdType.MESH
F32, BF16 = jnp.float32, jnp.bfloat16

ROWS, COLS, RANK = 4096, 128, 64
HALF = ROWS // 2
PART = ROWS // 4
NY, NX, NZ = 4, 2, 8
BIG = (48, 32, 32)
SMALL = (8, 8)
SIZES = BIG + SMALL
NB, NS, NC = len(BIG), len(SMALL), len(SIZES)
NT = NB - 1
FIRST = tuple(sum(SIZES[:k]) for k in range(NC))
BLK = 512


def split(v):
    hi = v.astype(BF16)
    return hi, (v - hi.astype(F32)).astype(BF16)


def dot(a, b):
    return jnp.dot(a, b, preferred_element_type=F32)


def dot3(a, b_hi, b_lo):
    m = a.shape[0]
    hi = a.astype(BF16).astype(F32)
    both = dot(jnp.concatenate([hi, a - hi], 0).astype(BF16), b_hi)
    return both[:m] + both[m:] + dot(hi.astype(BF16), b_lo)


def kernel(scale, x_hbm, f_ref, gram_ref, core_ref, *scratch):
    scratch = list(scratch)

    def take(n=None):
        if n is None:
            return scratch.pop(0)
        return [scratch.pop(0) for _ in range(n)]

    nat, pnat, st, xt, ft, abh, abl, eacc, tt, tr = take(10)
    rt, p1, zb = take(NB + 1), take(NB + 1), take(NB + 1)
    wb, rp, qb = take(NB), take(NB), take(NB)
    px, qx = take(NT), take(NT)
    ex, eb = take(2)
    z2, w2, rp2, qb2 = take(NS), take(NS), take(NS), take(NS)
    ld, cs, cr, fs, fr, xs, xr, s1, r1, s2, r2, s3, r3, s4, r4, s5, r5, s6, r6, ts, trs = take(21)

    s, p = lax.axis_index("span"), lax.axis_index("plane")
    l, c = s // 2, s % 2
    z = p % NZ
    x = (p // NZ) % NX
    y = p // (NZ * NX)
    h, v = y // 2, y % 2

    def dev(l, c, y, x, z):
        return {"span": l * 2 + c, "plane": (y * NX + x) * NZ + z}

    def yy(k):
        return lax.rem(y + k, NY)

    def zz(k):
        return lax.rem(z + k, NZ)

    def place(k):
        return yy(k + 1), lax.rem(x + 1 + k // NY, NX)

    def each(first, last, do):
        def step(k, _):
            do(k)
            return 0

        lax.fori_loop(first, last, step, 0)

    here_last = NX * NY - 1
    w = x * NY + y

    def remote(src, dst, send, recv, to):
        return pltpu.make_async_remote_copy(
            src_ref=src, dst_ref=dst, send_sem=send, recv_sem=recv, device_id=to, device_id_type=MESH
        )

    def wait_bytes(ref, sem):
        pltpu.make_async_copy(ref, ref, sem).wait()

    barrier = pltpu.get_barrier_semaphore()

    def greet(*to):
        pl.semaphore_signal(barrier, inc=1, device_id=dev(*to), device_id_type=MESH)

    def greet_places(k):
        greet(1 - l, c, *place(k), z)
        greet(l, 1 - c, *place(k), z)

    each(0, NX * NY, greet_places)
    each(0, here_last, lambda k: greet(l, c, *place(k), z))
    each(1, NZ, lambda k: greet(l, c, y, x, zz(k)))

    here = [pl.ds(pl.multiple_of((1 - l) * HALF, HALF), HALF), pl.ds(pl.multiple_of(l * HALF, HALF), HALF)]
    loads = [pltpu.make_async_copy(x_hbm.at[here[i]], nat.at[i], ld.at[i]) for i in range(2)]
    loads[0].start()
    loads[1].start()
    ft[0] = f_ref[...]

    def turn(i):
        def step(b, _):
            at = pl.ds(pl.multiple_of(b * 128, 128), 128)
            st[i, :, at] = nat[i, at, :].T
            return 0

        lax.fori_loop(0, HALF // 128, step, 0, unroll=2)

    loads[0].wait()
    turn(0)
    pl.semaphore_wait(barrier, 3 * NY * NX - 1 + NZ - 1)

    xpeer, cpeer = dev(1 - l, c, y, x, z), dev(l, 1 - c, y, x, z)
    chunk = [pl.ds(FIRST[k], SIZES[k]) for k in range(NC)]
    xcopy = [remote(st.at[0, chunk[k]], xt.at[chunk[k]], xs.at[k], xr.at[k], xpeer) for k in range(NC)]
    ccopy = [remote(x_hbm.at[here[i]], pnat.at[i], cs.at[i], cr.at[i], cpeer) for i in range(2)]
    fcopy = remote(ft.at[0], ft.at[1], fs, fr, xpeer)
    xcopy[0].start()
    ccopy[1].start()
    for k in range(1, NC):
        xcopy[k].start()
    ccopy[0].start()
    fcopy.start()
    loads[1].wait()
    turn(1)

    def inchip(i, keep):
        def step(b, _):
            at = pl.ds(pl.multiple_of(b * BLK, BLK), BLK)
            ab_hi, ab_lo = split(jnp.concatenate([nat[i, at, :], pnat[i, at, :]], 1))
            if keep:
                abh[at, :] = ab_hi
                abl[at, :] = ab_lo
            eacc[...] += dot3(st[i, :, at], ab_hi, ab_lo)
            return 0

        lax.fori_loop(0, HALF // BLK, step, 0)

    def scatter(k, slab):
        n = slab.shape[0] // 2
        for half in range(2):
            rt[k][c * 2 + half] = slab[half * n : half * n + n, :128]
            rt[k][(1 - c) * 2 + half] = slab[half * n : half * n + n, 128:]
        for j in (2, 1, 3):
            remote(rt[k].at[yy(j)], p1[k].at[j - 1], s1.at[k], r1.at[k], dev(l, c, yy(j), x, z)).start()

    def sum_y(k):
        wait_bytes(p1[k], r1.at[k])
        zb[k][z] = rt[k][y] + p1[k][0] + p1[k][1] + p1[k][2]
        each(1, NZ, lambda j: remote(zb[k].at[z], zb[k].at[z], s2.at[k], r2.at[k], dev(l, c, y, x, zz(j))).start())

    def sum_z(ref, k):
        wait_bytes(ref.at[pl.ds(0, NZ - 1)], r2.at[k])
        total = ref[0]
        for j in range(1, NZ):
            total += ref[j]
        return total

    def gather(k):
        wb[k][...] = sum_z(zb[k], k)
        mine = qb[k].at[c, x * 2 + v]
        each(0, NX * NY, lambda o: remote(wb[k], rp[k].at[w], s3.at[k], r3.at[k], dev(1 - l, c, *place(o), z)).start())
        each(0, here_last, lambda o: remote(wb[k], mine, s4.at[k], r4.at[k], dev(l, h, *place(o), z)).start())

        @pl.when(h == c)
        def _():
            pltpu.make_async_copy(wb[k], mine, r4.at[k]).start()

        @pl.when(h != c)
        def _():
            remote(wb[k], mine, s4.at[k], r4.at[k], dev(l, h, y, x, z)).start()

    def gather_x(k):
        wb[k][...] = sum_z(zb[k], k)
        each(0, NX, lambda o: remote(wb[k], px[k].at[x], s3.at[k], r3.at[k], dev(1 - l, c, y, o, z)).start())
        mine = qx[k].at[c * NX + x]
        remote(wb[k], mine, s4.at[k], r4.at[k], dev(l, h, y, 1 - x, z)).start()

        @pl.when(h == c)
        def _():
            pltpu.make_async_copy(wb[k], mine, r4.at[k]).start()

        @pl.when(h != c)
        def _():
            remote(wb[k], mine, s4.at[k], r4.at[k], dev(l, h, y, x, z)).start()

    def gather_y(k):
        wait_bytes(px[k], r3.at[k])
        rp[k][y] = px[k][0] + px[k][1]
        each(1, NY, lambda j: remote(rp[k].at[y], rp[k].at[y], s5.at[k], r5.at[k], dev(l, c, yy(j), x, z)).start())

        @pl.when(h == c)
        def _():
            wait_bytes(qx[k], r4.at[k])
            qb[k][v, 0] = qx[k][0] + qx[k][1]
            qb[k][v, 1] = qx[k][2] + qx[k][3]
            each(1, NY, lambda j: remote(qb[k].at[v], qb[k].at[v], s6.at[k], r6.at[k], dev(l, c, yy(j), x, z)).start())

    def gathered(k):
        wait_bytes(rp[k].at[pl.ds(0, NY - 1)], r5.at[k])

        @pl.when(h == c)
        def _():
            wait_bytes(qb[k].at[0], r6.at[k])

        @pl.when(h != c)
        def _():
            wait_bytes(qb[k], r6.at[k])

    def inchip_x():
        ex[x] = sum_z(zb[NB], NB)
        remote(ex.at[x], ex.at[x], s3.at[NC], r3.at[NC], dev(l, c, y, 1 - x, z)).start()

    def inchip_y():
        wait_bytes(ex.at[0], r3.at[NC])
        eb[y] = ex[0] + ex[1]
        each(1, NY, lambda j: remote(eb.at[y], eb.at[y], s5.at[NT], r5.at[NT], dev(l, c, yy(j), x, z)).start())

    def slab_of(k):
        xcopy[k].wait_recv()

        def step(b, total):
            at = pl.ds(pl.multiple_of(b * BLK, BLK), BLK)
            return total + dot3(xt[chunk[k], at], abh[at, :], abl[at, :])

        return lax.fori_loop(0, HALF // BLK, step, jnp.zeros((SIZES[k], 2 * COLS), F32))

    def spread_z(i):
        k = NB + i
        slab = slab_of(k)
        z2[i][z, c] = slab[:, :128]
        z2[i][z, 1 - c] = slab[:, 128:]
        each(1, NZ, lambda j: remote(z2[i].at[z], z2[i].at[z], s2.at[k + 1], r2.at[k + 1], dev(l, c, y, x, zz(j))).start())

    def spread_xy(i):
        k = NB + i
        w2[i][...] = sum_z(z2[i], k + 1)
        mine = qb2[i].at[c * NX * NY + w]

        def send(o):
            to = place(o)
            remote(w2[i], rp2[i].at[w], s3.at[k], r3.at[k], dev(1 - l, c, *to, z)).start()
            remote(w2[i].at[1 - c], mine, s4.at[k], r4.at[k], dev(l, 1 - c, *to, z)).start()

        each(0, NX * NY, send)
        each(0, here_last, lambda o: remote(w2[i].at[c], mine, s4.at[k], r4.at[k], dev(l, c, *place(o), z)).start())
        pltpu.make_async_copy(w2[i].at[c], mine, r4.at[k]).start()

    eacc[...] = jnp.zeros_like(eacc)
    ccopy[1].wait_recv()
    inchip(1, True)
    ccopy[0].wait_recv()
    inchip(0, False)
    scatter(NB, eacc[...])
    scatter(0, slab_of(0))
    sum_y(NB)
    sum_y(0)
    scatter(1, slab_of(1))
    inchip_x()
    sum_y(1)
    gather_x(0)
    scatter(2, slab_of(2))
    spread_z(0)
    spread_z(1)
    sum_y(2)
    inchip_y()
    gather_y(0)
    gather_x(1)

    fcopy.wait_recv()
    f_hi, f_lo = split(jnp.concatenate([ft[0], ft[1]], 1))
    f_both = jnp.concatenate([f_hi, f_lo], 0)

    def project(b, _):
        at = pl.ds(pl.multiple_of(b * 256, 256), 256)
        v_hi, v_lo = split(jnp.concatenate([st[1, :, at], xt[:, at]], 0))
        both = dot(f_both, v_hi)
        to = pl.ds(pl.multiple_of(b % 4 * 256, 256), 256)
        tt[b // 4, :, to] = both[:RANK] + both[RANK:] + dot(f_hi, v_lo)
        return 0

    lax.fori_loop(0, HALF // 256, project, 0)
    tcopy = remote(tt.at[1 - c], tr, ts, trs, cpeer)
    tcopy.start()

    spread_xy(0)
    spread_xy(1)
    gather(2)
    gather_y(1)

    tcopy.wait_recv()
    core_ref[...] = tt[c] + tr[...]
    wait_bytes(eb.at[pl.ds(0, NY - 1)], r5.at[NT])
    for q in range(2):
        at = pl.ds(pl.multiple_of(l * 256 + q * 128, 128), 128)
        gram_ref[:, at] = jnp.concatenate([eb[q * 2 + i] * scale for i in range(2)], 0)

    for k in range(NC):
        if k < NT:
            gathered(k)
        else:
            wait_bytes(rp[k] if k < NB else rp2[k - NB], r3.at[k])
            wait_bytes(qb[k] if k < NB else qb2[k - NB], r4.at[k])

    def all_places(pieces):
        total = pieces[0]
        for piece in pieces[1:]:
            total += piece
        return total

    for q in range(2):
        direct, turned = [], []
        for k in range(NB):
            for i in range(2):
                if k < NT:
                    direct.append(rp[k][q * 2 + i])
                    turned.append(qb[k][i, q])
                else:
                    direct.append(rp[k][q * 2 + i] + rp[k][NY + q * 2 + i])
                    turned.append(qb[k][q, i] + qb[k][q, 2 + i])
        for i in range(NS):
            direct.append(all_places([rp2[i][j, q] for j in range(NX * NY)]))
            turned.append(all_places([qb2[i][q * NX * NY + j] for j in range(NX * NY)]))
        at = pl.ds(pl.multiple_of((1 - l) * 256 + q * 128, 128), 128)
        gram_ref[:, at] = (jnp.concatenate(direct, 0) + jnp.concatenate(turned, 0).T) * scale

    for i in range(2):
        ccopy[i].wait_send()
    fcopy.wait_send()
    tcopy.wait_send()
    for k in range(NC):
        xcopy[k].wait_send()
    for k in range(NB + 1):
        wait_bytes(p1[k], s1.at[k])
        wait_bytes(zb[k].at[pl.ds(0, NZ - 1)], s2.at[k])
    for k in range(NB):
        pieces = px[k] if k < NT else rp[k]
        wait_bytes(pieces, s3.at[k])

        @pl.when(h == c)
        def _():
            wait_bytes(pieces.at[pl.ds(0, pieces.shape[0] - 1)], s4.at[k])

        @pl.when(h != c)
        def _():
            wait_bytes(pieces, s4.at[k])

        if k < NT:
            wait_bytes(rp[k].at[pl.ds(0, NY - 1)], s5.at[k])

            @pl.when(h == c)
            def _():
                wait_bytes(zb[k].at[pl.ds(0, 2 * (NY - 1))], s6.at[k])

    wait_bytes(ex.at[0], s3.at[NC])
    wait_bytes(eb.at[pl.ds(0, NY - 1)], s5.at[NT])
    for i in range(NS):
        k = NB + i
        wait_bytes(z2[i].at[pl.ds(0, NZ - 1)], s2.at[k + 1])
        wait_bytes(rp2[i], s3.at[k])
        wait_bytes(qb2[i].at[pl.ds(0, 2 * NX * NY - 1)], s4.at[k])


def write(gram_ref, core_ref, gram_out, core_out):
    gram_out[...] = gram_ref[...]
    core_out[...] = core_ref[...]


def local(snapshot, factor):
    fibres = snapshot.shape[0] * lax.axis_size("plane")
    dma = pltpu.SemaphoreType.DMA

    def vmem(*shape, dtype=F32):
        return pltpu.VMEM(shape, dtype)

    pieces = [n // 2 for n in BIG]
    with_e = pieces + [COLS // 2]
    outs = [((COLS, 4 * COLS), F32), ((RANK, PART), F32)]
    made = pl.pallas_call(
        functools.partial(kernel, 1.0 / fibres),
        out_shape=[jax.ShapeDtypeStruct(*o) for o in outs],
        in_specs=[pl.BlockSpec(memory_space=pl.ANY), pl.BlockSpec(memory_space=pltpu.VMEM)],
        out_specs=[pl.BlockSpec(memory_space=pltpu.VMEM)] * 2,
        scratch_shapes=[
            vmem(2, HALF, COLS),
            vmem(2, HALF, COLS),
            vmem(2, COLS, HALF),
            vmem(COLS, HALF),
            vmem(2, RANK, COLS),
            vmem(HALF, 2 * COLS, dtype=BF16),
            vmem(HALF, 2 * COLS, dtype=BF16),
            vmem(COLS, 2 * COLS),
            vmem(2, RANK, PART),
            vmem(RANK, PART),
        ]
        + [vmem(NY, n, 128) for n in with_e]
        + [vmem(NY - 1, n, 128) for n in with_e]
        + [vmem(NZ, n, 128) for n in with_e]
        + [vmem(n, 128) for n in pieces]
        + [vmem(NY, n, 128) for n in pieces[:NT]]
        + [vmem(NX * NY, n, 128) for n in pieces[NT:]]
        + [vmem(2, 2, n, 128) for n in pieces[:NT]]
        + [vmem(2, NX * 2, n, 128) for n in pieces[NT:]]
        + [vmem(NX, n, 128) for n in pieces[:NT]]
        + [vmem(2 * NX, n, 128) for n in pieces[:NT]]
        + [vmem(NX, COLS // 2, 128), vmem(NY, COLS // 2, 128)]
        + [vmem(NZ, 2, n, 128) for n in SMALL]
        + [vmem(2, n, 128) for n in SMALL]
        + [vmem(NX * NY, 2, n, 128) for n in SMALL]
        + [vmem(2 * NX * NY, n, 128) for n in SMALL]
        + [dma((2,)), dma((2,)), dma((2,)), dma, dma, dma((NC,)), dma((NC,))]
        + [dma((NB + 1,)), dma((NB + 1,)), dma((NC + 1,)), dma((NC + 1,))]
        + [dma((NC + 1,)), dma((NC + 1,)), dma((NC,)), dma((NC,))]
        + [dma((NT + 1,)), dma((NT + 1,)), dma((NT,)), dma((NT,)), dma, dma],
        compiler_params=pltpu.CompilerParams(
            collective_id=0, has_side_effects=True, vmem_limit_bytes=60 * 2**20
        ),
    )(snapshot, factor.T)
    return pl.pallas_call(
        write,
        out_shape=[jax.ShapeDtypeStruct(*o) for o in outs],
    )(*made)


def solution(mesh):
    return jax.shard_map(
        local,
        mesh=mesh,
        in_specs=(P("plane", "span"), P("span", None)),
        out_specs=(P("span", None), P(None, ("plane", "span"))),
        check_vma=False,
    )
```

```python
import functools

import jax
import jax.numpy as jnp
from jax import lax
from jax.experimental import pallas as pl
from jax.experimental.pallas import tpu as pltpu
from jax.sharding import PartitionSpec as P

MESH = pl.DeviceIdType.MESH
F32, BF16 = jnp.float32, jnp.bfloat16

ROWS, COLS, RANK = 4096, 128, 64
HALF = ROWS // 2
PART = ROWS // 4
NY, NX, NZ = 4, 2, 8
BIG = (48, 32, 32)
SMALL = (8, 8)
SIZES = BIG + SMALL
NB, NS, NC = len(BIG), len(SMALL), len(SIZES)
NT = NB - 1
FIRST = tuple(sum(SIZES[:k]) for k in range(NC))
BLK = 512


def split(v):
    hi = v.astype(BF16)
    return hi, (v - hi.astype(F32)).astype(BF16)


def dot(a, b):
    return jnp.dot(a, b, preferred_element_type=F32)


def dot3(a, b_hi, b_lo):
    m = a.shape[0]
    hi = a.astype(BF16).astype(F32)
    both = dot(jnp.concatenate([hi, a - hi], 0).astype(BF16), b_hi)
    return both[:m] + both[m:] + dot(hi.astype(BF16), b_lo)


def kernel(scale, x_hbm, f_ref, gram_ref, core_ref, *scratch):
    scratch = list(scratch)

    def take(n=None):
        if n is None:
            return scratch.pop(0)
        return [scratch.pop(0) for _ in range(n)]

    nat, pnat, st, xt, ft, abh, abl, eacc, tt, tr = take(10)
    rt, p1, zb = take(NB + 1), take(NB + 1), take(NB + 1)
    wb, rp, qb = take(NB), take(NB), take(NB)
    px, qx = take(NT), take(NT)
    ex, eb = take(2)
    z2, w2, rp2, qb2 = take(NS), take(NS), take(NS), take(NS)
    ld, cs, cr, fs, fr, xs, xr, s1, r1, s2, r2, s3, r3, s4, r4, s5, r5, s6, r6, ts, trs = take(21)

    s, p = lax.axis_index("span"), lax.axis_index("plane")
    l, c = s // 2, s % 2
    z = p % NZ
    x = (p // NZ) % NX
    y = p // (NZ * NX)
    h, v = y // 2, y % 2

    def dev(l, c, y, x, z):
        return {"span": l * 2 + c, "plane": (y * NX + x) * NZ + z}

    def yy(k):
        return lax.rem(y + k, NY)

    def yfar(k):
        return lax.rem(y + 2 + k // 2 * (1 - k % 2 * 2) + NY, NY)

    def zz(k):
        return lax.rem(z + NZ // 2 + k // 2 * (1 - k % 2 * 2) + NZ, NZ)

    def place(k):
        return yfar(1 + k % NY), lax.rem(x + 1 + k // NY, NX)

    def each(first, last, do):
        def step(k, _):
            do(k)
            return 0

        lax.fori_loop(first, last, step, 0)

    here_last = NX * NY - 1
    w = x * NY + y

    def remote(src, dst, send, recv, to):
        return pltpu.make_async_remote_copy(
            src_ref=src, dst_ref=dst, send_sem=send, recv_sem=recv, device_id=to, device_id_type=MESH
        )

    def wait_bytes(ref, sem):
        pltpu.make_async_copy(ref, ref, sem).wait()

    barrier = pltpu.get_barrier_semaphore()

    def greet(*to):
        pl.semaphore_signal(barrier, inc=1, device_id=dev(*to), device_id_type=MESH)

    def greet_places(k):
        greet(1 - l, c, *place(k), z)
        greet(l, 1 - c, *place(k), z)

    each(0, NX * NY, greet_places)
    each(0, here_last, lambda k: greet(l, c, *place(k), z))
    each(1, NZ, lambda k: greet(l, c, y, x, zz(k)))

    here = [pl.ds(pl.multiple_of((1 - l) * HALF, HALF), HALF), pl.ds(pl.multiple_of(l * HALF, HALF), HALF)]
    loads = [pltpu.make_async_copy(x_hbm.at[here[i]], nat.at[i], ld.at[i]) for i in range(2)]
    loads[0].start()
    loads[1].start()
    ft[0] = f_ref[...]

    def turn(i):
        def step(b, _):
            at = pl.ds(pl.multiple_of(b * 128, 128), 128)
            st[i, :, at] = nat[i, at, :].T
            return 0

        lax.fori_loop(0, HALF // 128, step, 0, unroll=2)

    loads[0].wait()
    turn(0)
    pl.semaphore_wait(barrier, 3 * NY * NX - 1 + NZ - 1)

    xpeer, cpeer = dev(1 - l, c, y, x, z), dev(l, 1 - c, y, x, z)
    chunk = [pl.ds(FIRST[k], SIZES[k]) for k in range(NC)]
    xcopy = [remote(st.at[0, chunk[k]], xt.at[chunk[k]], xs.at[k], xr.at[k], xpeer) for k in range(NC)]
    ccopy = [remote(x_hbm.at[here[i]], pnat.at[i], cs.at[i], cr.at[i], cpeer) for i in range(2)]
    fcopy = remote(ft.at[0], ft.at[1], fs, fr, xpeer)
    xcopy[0].start()
    ccopy[1].start()
    for k in range(1, NC):
        xcopy[k].start()
    ccopy[0].start()
    fcopy.start()
    loads[1].wait()
    turn(1)

    def inchip(i, keep):
        def step(b, _):
            at = pl.ds(pl.multiple_of(b * BLK, BLK), BLK)
            ab_hi, ab_lo = split(jnp.concatenate([nat[i, at, :], pnat[i, at, :]], 1))
            if keep:
                abh[at, :] = ab_hi
                abl[at, :] = ab_lo
            eacc[...] += dot3(st[i, :, at], ab_hi, ab_lo)
            return 0

        lax.fori_loop(0, HALF // BLK, step, 0)

    def scatter(k, slab):
        n = slab.shape[0] // 2
        for half in range(2):
            rt[k][c * 2 + half] = slab[half * n : half * n + n, :128]
            rt[k][(1 - c) * 2 + half] = slab[half * n : half * n + n, 128:]
        for j in (2, 1, 3):
            remote(rt[k].at[yy(j)], p1[k].at[j - 1], s1.at[k], r1.at[k], dev(l, c, yy(j), x, z)).start()

    def sum_y(k):
        wait_bytes(p1[k], r1.at[k])
        zb[k][z] = rt[k][y] + p1[k][0] + p1[k][1] + p1[k][2]
        each(1, NZ, lambda j: remote(zb[k].at[z], zb[k].at[z], s2.at[k], r2.at[k], dev(l, c, y, x, zz(j))).start())

    def sum_z(ref, k):
        wait_bytes(ref.at[pl.ds(0, NZ - 1)], r2.at[k])
        total = ref[0]
        for j in range(1, NZ):
            total += ref[j]
        return total

    def gather(k):
        wb[k][...] = sum_z(zb[k], k)
        mine = qb[k].at[c, x * 2 + v]
        each(0, NX * NY, lambda o: remote(wb[k], rp[k].at[w], s3.at[k], r3.at[k], dev(1 - l, c, *place(o), z)).start())
        each(0, here_last, lambda o: remote(wb[k], mine, s4.at[k], r4.at[k], dev(l, h, *place(o), z)).start())

        @pl.when(h == c)
        def _():
            pltpu.make_async_copy(wb[k], mine, r4.at[k]).start()

        @pl.when(h != c)
        def _():
            remote(wb[k], mine, s4.at[k], r4.at[k], dev(l, h, y, x, z)).start()

    def gather_x(k):
        wb[k][...] = sum_z(zb[k], k)
        each(0, NX, lambda o: remote(wb[k], px[k].at[x], s3.at[k], r3.at[k], dev(1 - l, c, y, o, z)).start())
        mine = qx[k].at[c * NX + x]
        remote(wb[k], mine, s4.at[k], r4.at[k], dev(l, h, y, 1 - x, z)).start()

        @pl.when(h == c)
        def _():
            pltpu.make_async_copy(wb[k], mine, r4.at[k]).start()

        @pl.when(h != c)
        def _():
            remote(wb[k], mine, s4.at[k], r4.at[k], dev(l, h, y, x, z)).start()

    def gather_y(k):
        wait_bytes(px[k], r3.at[k])
        rp[k][y] = px[k][0] + px[k][1]
        each(1, NY, lambda j: remote(rp[k].at[y], rp[k].at[y], s5.at[k], r5.at[k], dev(l, c, yfar(j), x, z)).start())

        @pl.when(h == c)
        def _():
            wait_bytes(qx[k], r4.at[k])
            qb[k][v, 0] = qx[k][0] + qx[k][1]
            qb[k][v, 1] = qx[k][2] + qx[k][3]
            each(1, NY, lambda j: remote(qb[k].at[v], qb[k].at[v], s6.at[k], r6.at[k], dev(l, c, yy(j), x, z)).start())

    def gathered(k):
        wait_bytes(rp[k].at[pl.ds(0, NY - 1)], r5.at[k])

        @pl.when(h == c)
        def _():
            wait_bytes(qb[k].at[0], r6.at[k])

        @pl.when(h != c)
        def _():
            wait_bytes(qb[k], r6.at[k])

    def inchip_x():
        ex[x] = sum_z(zb[NB], NB)
        remote(ex.at[x], ex.at[x], s3.at[NC], r3.at[NC], dev(l, c, y, 1 - x, z)).start()

    def inchip_y():
        wait_bytes(ex.at[0], r3.at[NC])
        eb[y] = ex[0] + ex[1]
        each(1, NY, lambda j: remote(eb.at[y], eb.at[y], s5.at[NT], r5.at[NT], dev(l, c, yy(j), x, z)).start())

    def slab_of(k):
        xcopy[k].wait_recv()

        def step(b, total):
            at = pl.ds(pl.multiple_of(b * BLK, BLK), BLK)
            return total + dot3(xt[chunk[k], at], abh[at, :], abl[at, :])

        return lax.fori_loop(0, HALF // BLK, step, jnp.zeros((SIZES[k], 2 * COLS), F32))

    def spread_z(i):
        k = NB + i
        slab = slab_of(k)
        z2[i][z, c] = slab[:, :128]
        z2[i][z, 1 - c] = slab[:, 128:]
        each(1, NZ, lambda j: remote(z2[i].at[z], z2[i].at[z], s2.at[k + 1], r2.at[k + 1], dev(l, c, y, x, zz(j))).start())

    def spread_xy(i):
        k = NB + i
        w2[i][...] = sum_z(z2[i], k + 1)
        mine = qb2[i].at[c * NX * NY + w]

        def send(o):
            to = place(o)
            remote(w2[i], rp2[i].at[w], s3.at[k], r3.at[k], dev(1 - l, c, *to, z)).start()
            remote(w2[i].at[1 - c], mine, s4.at[k], r4.at[k], dev(l, 1 - c, *to, z)).start()

        each(0, NX * NY, send)
        each(0, here_last, lambda o: remote(w2[i].at[c], mine, s4.at[k], r4.at[k], dev(l, c, *place(o), z)).start())
        pltpu.make_async_copy(w2[i].at[c], mine, r4.at[k]).start()

    eacc[...] = jnp.zeros_like(eacc)
    ccopy[1].wait_recv()
    inchip(1, True)
    ccopy[0].wait_recv()
    inchip(0, False)
    scatter(NB, eacc[...])
    scatter(0, slab_of(0))
    sum_y(NB)
    sum_y(0)
    scatter(1, slab_of(1))
    inchip_x()
    sum_y(1)
    gather_x(0)
    scatter(2, slab_of(2))
    spread_z(0)
    spread_z(1)
    sum_y(2)
    inchip_y()
    gather_y(0)
    gather_x(1)

    fcopy.wait_recv()
    f_hi, f_lo = split(jnp.concatenate([ft[0], ft[1]], 1))
    f_both = jnp.concatenate([f_hi, f_lo], 0)

    def project(b, _):
        at = pl.ds(pl.multiple_of(b * 256, 256), 256)
        v_hi, v_lo = split(jnp.concatenate([st[1, :, at], xt[:, at]], 0))
        both = dot(f_both, v_hi)
        to = pl.ds(pl.multiple_of(b % 4 * 256, 256), 256)
        tt[b // 4, :, to] = both[:RANK] + both[RANK:] + dot(f_hi, v_lo)
        return 0

    lax.fori_loop(0, HALF // 256, project, 0)
    tcopy = remote(tt.at[1 - c], tr, ts, trs, cpeer)
    tcopy.start()

    spread_xy(0)
    spread_xy(1)
    gather(2)
    gather_y(1)

    tcopy.wait_recv()
    core_ref[...] = tt[c] + tr[...]
    wait_bytes(eb.at[pl.ds(0, NY - 1)], r5.at[NT])
    for q in range(2):
        at = pl.ds(pl.multiple_of(l * 256 + q * 128, 128), 128)
        gram_ref[:, at] = jnp.concatenate([eb[q * 2 + i] * scale for i in range(2)], 0)

    for k in range(NC):
        if k < NT:
            gathered(k)
        else:
            wait_bytes(rp[k] if k < NB else rp2[k - NB], r3.at[k])
            wait_bytes(qb[k] if k < NB else qb2[k - NB], r4.at[k])

    def all_places(pieces):
        total = pieces[0]
        for piece in pieces[1:]:
            total += piece
        return total

    for q in range(2):
        direct, turned = [], []
        for k in range(NB):
            for i in range(2):
                if k < NT:
                    direct.append(rp[k][q * 2 + i])
                    turned.append(qb[k][i, q])
                else:
                    direct.append(rp[k][q * 2 + i] + rp[k][NY + q * 2 + i])
                    turned.append(qb[k][q, i] + qb[k][q, 2 + i])
        for i in range(NS):
            direct.append(all_places([rp2[i][j, q] for j in range(NX * NY)]))
            turned.append(all_places([qb2[i][q * NX * NY + j] for j in range(NX * NY)]))
        at = pl.ds(pl.multiple_of((1 - l) * 256 + q * 128, 128), 128)
        gram_ref[:, at] = (jnp.concatenate(direct, 0) + jnp.concatenate(turned, 0).T) * scale

    for i in range(2):
        ccopy[i].wait_send()
    fcopy.wait_send()
    tcopy.wait_send()
    for k in range(NC):
        xcopy[k].wait_send()
    for k in range(NB + 1):
        wait_bytes(p1[k], s1.at[k])
        wait_bytes(zb[k].at[pl.ds(0, NZ - 1)], s2.at[k])
    for k in range(NB):
        pieces = px[k] if k < NT else rp[k]
        wait_bytes(pieces, s3.at[k])

        @pl.when(h == c)
        def _():
            wait_bytes(pieces.at[pl.ds(0, pieces.shape[0] - 1)], s4.at[k])

        @pl.when(h != c)
        def _():
            wait_bytes(pieces, s4.at[k])

        if k < NT:
            wait_bytes(rp[k].at[pl.ds(0, NY - 1)], s5.at[k])

            @pl.when(h == c)
            def _():
                wait_bytes(zb[k].at[pl.ds(0, 2 * (NY - 1))], s6.at[k])

    wait_bytes(ex.at[0], s3.at[NC])
    wait_bytes(eb.at[pl.ds(0, NY - 1)], s5.at[NT])
    for i in range(NS):
        k = NB + i
        wait_bytes(z2[i].at[pl.ds(0, NZ - 1)], s2.at[k + 1])
        wait_bytes(rp2[i], s3.at[k])
        wait_bytes(qb2[i].at[pl.ds(0, 2 * NX * NY - 1)], s4.at[k])


def write(gram_ref, core_ref, gram_out, core_out):
    gram_out[...] = gram_ref[...]
    core_out[...] = core_ref[...]


def local(snapshot, factor):
    fibres = snapshot.shape[0] * lax.axis_size("plane")
    dma = pltpu.SemaphoreType.DMA

    def vmem(*shape, dtype=F32):
        return pltpu.VMEM(shape, dtype)

    pieces = [n // 2 for n in BIG]
    with_e = pieces + [COLS // 2]
    outs = [((COLS, 4 * COLS), F32), ((RANK, PART), F32)]
    made = pl.pallas_call(
        functools.partial(kernel, 1.0 / fibres),
        out_shape=[jax.ShapeDtypeStruct(*o) for o in outs],
        in_specs=[pl.BlockSpec(memory_space=pl.ANY), pl.BlockSpec(memory_space=pltpu.VMEM)],
        out_specs=[pl.BlockSpec(memory_space=pltpu.VMEM)] * 2,
        scratch_shapes=[
            vmem(2, HALF, COLS),
            vmem(2, HALF, COLS),
            vmem(2, COLS, HALF),
            vmem(COLS, HALF),
            vmem(2, RANK, COLS),
            vmem(HALF, 2 * COLS, dtype=BF16),
            vmem(HALF, 2 * COLS, dtype=BF16),
            vmem(COLS, 2 * COLS),
            vmem(2, RANK, PART),
            vmem(RANK, PART),
        ]
        + [vmem(NY, n, 128) for n in with_e]
        + [vmem(NY - 1, n, 128) for n in with_e]
        + [vmem(NZ, n, 128) for n in with_e]
        + [vmem(n, 128) for n in pieces]
        + [vmem(NY, n, 128) for n in pieces[:NT]]
        + [vmem(NX * NY, n, 128) for n in pieces[NT:]]
        + [vmem(2, 2, n, 128) for n in pieces[:NT]]
        + [vmem(2, NX * 2, n, 128) for n in pieces[NT:]]
        + [vmem(NX, n, 128) for n in pieces[:NT]]
        + [vmem(2 * NX, n, 128) for n in pieces[:NT]]
        + [vmem(NX, COLS // 2, 128), vmem(NY, COLS // 2, 128)]
        + [vmem(NZ, 2, n, 128) for n in SMALL]
        + [vmem(2, n, 128) for n in SMALL]
        + [vmem(NX * NY, 2, n, 128) for n in SMALL]
        + [vmem(2 * NX * NY, n, 128) for n in SMALL]
        + [dma((2,)), dma((2,)), dma((2,)), dma, dma, dma((NC,)), dma((NC,))]
        + [dma((NB + 1,)), dma((NB + 1,)), dma((NC + 1,)), dma((NC + 1,))]
        + [dma((NC + 1,)), dma((NC + 1,)), dma((NC,)), dma((NC,))]
        + [dma((NT + 1,)), dma((NT + 1,)), dma((NT,)), dma((NT,)), dma, dma],
        compiler_params=pltpu.CompilerParams(
            collective_id=0, has_side_effects=True, vmem_limit_bytes=60 * 2**20
        ),
    )(snapshot, factor.T)
    return pl.pallas_call(
        write,
        out_shape=[jax.ShapeDtypeStruct(*o) for o in outs],
    )(*made)


def solution(mesh):
    return jax.shard_map(
        local,
        mesh=mesh,
        in_specs=(P("plane", "span"), P("span", None)),
        out_specs=(P("span", None), P(None, ("plane", "span"))),
        check_vma=False,
    )
```

```python
import functools

import jax
import jax.numpy as jnp
from jax import lax
from jax.experimental import pallas as pl
from jax.experimental.pallas import tpu as pltpu
from jax.sharding import PartitionSpec as P

MESH = pl.DeviceIdType.MESH
F32, BF16 = jnp.float32, jnp.bfloat16

ROWS, COLS, RANK = 4096, 128, 64
HALF = ROWS // 2
PART = ROWS // 4
NY, NX, NZ = 4, 2, 8
BIG = (48, 32, 32)
SMALL = (8, 8)
SIZES = BIG + SMALL
NB, NS, NC = len(BIG), len(SMALL), len(SIZES)
NT = NB - 1
FIRST = tuple(sum(SIZES[:k]) for k in range(NC))
BLK = 512


def split(v):
    hi = v.astype(BF16)
    return hi, (v - hi.astype(F32)).astype(BF16)


def dot(a, b):
    return jnp.dot(a, b, preferred_element_type=F32)


def dot3(a, b_hi, b_lo):
    m = a.shape[0]
    hi = a.astype(BF16).astype(F32)
    both = dot(jnp.concatenate([hi, a - hi], 0).astype(BF16), b_hi)
    return both[:m] + both[m:] + dot(hi.astype(BF16), b_lo)


def kernel(scale, x_hbm, f_ref, gram_ref, core_ref, *scratch):
    scratch = list(scratch)

    def take(n=None):
        if n is None:
            return scratch.pop(0)
        return [scratch.pop(0) for _ in range(n)]

    nat, pnat, st, xt, ft, abh, abl, eacc, tt, tr = take(10)
    rt, p1, zb = take(NB + 1), take(NB + 1), take(NB + 1)
    wb, rp, qb = take(NB), take(NB), take(NB)
    px, qx = take(NT), take(NT)
    ex, eb = take(2)
    z2, w2, rp2, qb2 = take(NS), take(NS), take(NS), take(NS)
    ld, cs, cr, fs, fr, xs, xr, s1, r1, s2, r2, s3, r3, s4, r4, s5, r5, s6, r6, ts, trs = take(21)

    s, p = lax.axis_index("span"), lax.axis_index("plane")
    l, c = s // 2, s % 2
    z = p % NZ
    x = (p // NZ) % NX
    y = p // (NZ * NX)
    h, v = y // 2, y % 2

    def dev(l, c, y, x, z):
        return {"span": l * 2 + c, "plane": (y * NX + x) * NZ + z}

    def yy(k):
        return lax.rem(y + k, NY)

    def yfar(k):
        return lax.rem(y + 2 + k // 2 * (1 - k % 2 * 2) + NY, NY)

    def zz(k):
        return lax.rem(z + NZ // 2 + k // 2 * (1 - k % 2 * 2) + NZ, NZ)

    def place(k):
        return yfar(1 + k % NY), lax.rem(x + 1 + k // NY, NX)

    def each(first, last, do):
        def step(k, _):
            do(k)
            return 0

        lax.fori_loop(first, last, step, 0)

    here_last = NX * NY - 1
    w = x * NY + y

    def remote(src, dst, send, recv, to):
        return pltpu.make_async_remote_copy(
            src_ref=src, dst_ref=dst, send_sem=send, recv_sem=recv, device_id=to, device_id_type=MESH
        )

    def wait_bytes(ref, sem):
        pltpu.make_async_copy(ref, ref, sem).wait()

    barrier = pltpu.get_barrier_semaphore()

    def greet(*to):
        pl.semaphore_signal(barrier, inc=1, device_id=dev(*to), device_id_type=MESH)

    def greet_places(k):
        greet(1 - l, c, *place(k), z)
        greet(l, 1 - c, *place(k), z)

    each(0, NX * NY, greet_places)
    each(0, here_last, lambda k: greet(l, c, *place(k), z))
    each(1, NZ, lambda k: greet(l, c, y, x, zz(k)))

    here = [pl.ds(pl.multiple_of((1 - l) * HALF, HALF), HALF), pl.ds(pl.multiple_of(l * HALF, HALF), HALF)]
    loads = [pltpu.make_async_copy(x_hbm.at[here[i]], nat.at[i], ld.at[i]) for i in range(2)]
    loads[0].start()
    loads[1].start()
    ft[0] = f_ref[...]

    def turn(i):
        def step(b, _):
            at = pl.ds(pl.multiple_of(b * 128, 128), 128)
            st[i, :, at] = nat[i, at, :].T
            return 0

        lax.fori_loop(0, HALF // 128, step, 0, unroll=2)

    loads[0].wait()
    turn(0)
    pl.semaphore_wait(barrier, 3 * NY * NX - 1 + NZ - 1)

    xpeer, cpeer = dev(1 - l, c, y, x, z), dev(l, 1 - c, y, x, z)
    chunk = [pl.ds(FIRST[k], SIZES[k]) for k in range(NC)]
    xcopy = [remote(st.at[0, chunk[k]], xt.at[chunk[k]], xs.at[k], xr.at[k], xpeer) for k in range(NC)]
    ccopy = [remote(x_hbm.at[here[i]], pnat.at[i], cs.at[i], cr.at[i], cpeer) for i in range(2)]
    fcopy = remote(ft.at[0], ft.at[1], fs, fr, xpeer)
    xcopy[0].start()
    ccopy[1].start()
    for k in range(1, NC):
        xcopy[k].start()
    ccopy[0].start()
    fcopy.start()
    loads[1].wait()
    turn(1)

    def inchip(i, keep):
        def step(b, _):
            at = pl.ds(pl.multiple_of(b * BLK, BLK), BLK)
            ab_hi, ab_lo = split(jnp.concatenate([nat[i, at, :], pnat[i, at, :]], 1))
            if keep:
                abh[at, :] = ab_hi
                abl[at, :] = ab_lo
            eacc[...] += dot3(st[i, :, at], ab_hi, ab_lo)
            return 0

        lax.fori_loop(0, HALF // BLK, step, 0)

    def scatter(k, slab):
        n = slab.shape[0] // 2
        for half in range(2):
            rt[k][c * 2 + half] = slab[half * n : half * n + n, :128]
            rt[k][(1 - c) * 2 + half] = slab[half * n : half * n + n, 128:]
        for j in (2, 1, 3):
            remote(rt[k].at[yy(j)], p1[k].at[j - 1], s1.at[k], r1.at[k], dev(l, c, yy(j), x, z)).start()

    def sum_y(k):
        wait_bytes(p1[k], r1.at[k])
        zb[k][z] = rt[k][y] + p1[k][0] + p1[k][1] + p1[k][2]
        each(1, NZ, lambda j: remote(zb[k].at[z], zb[k].at[z], s2.at[k], r2.at[k], dev(l, c, y, x, zz(j))).start())

    def sum_z(ref, k):
        wait_bytes(ref.at[pl.ds(0, NZ - 1)], r2.at[k])
        total = ref[0]
        for j in range(1, NZ):
            total += ref[j]
        return total

    def gather(k):
        wb[k][...] = sum_z(zb[k], k)
        mine = qb[k].at[c, x * 2 + v]
        each(0, NX * NY, lambda o: remote(wb[k], rp[k].at[w], s3.at[k], r3.at[k], dev(1 - l, c, *place(o), z)).start())
        each(0, here_last, lambda o: remote(wb[k], mine, s4.at[k], r4.at[k], dev(l, h, *place(o), z)).start())

        @pl.when(h == c)
        def _():
            pltpu.make_async_copy(wb[k], mine, r4.at[k]).start()

        @pl.when(h != c)
        def _():
            remote(wb[k], mine, s4.at[k], r4.at[k], dev(l, h, y, x, z)).start()

    def gather_x(k):
        wb[k][...] = sum_z(zb[k], k)
        each(0, NX, lambda o: remote(wb[k], px[k].at[x], s3.at[k], r3.at[k], dev(1 - l, c, y, o, z)).start())
        mine = qx[k].at[c * NX + x]
        remote(wb[k], mine, s4.at[k], r4.at[k], dev(l, h, y, 1 - x, z)).start()

        @pl.when(h == c)
        def _():
            pltpu.make_async_copy(wb[k], mine, r4.at[k]).start()

        @pl.when(h != c)
        def _():
            remote(wb[k], mine, s4.at[k], r4.at[k], dev(l, h, y, x, z)).start()

    def gather_y(k):
        wait_bytes(px[k], r3.at[k])
        rp[k][y] = px[k][0] + px[k][1]
        each(1, NY, lambda j: remote(rp[k].at[y], rp[k].at[y], s5.at[k], r5.at[k], dev(l, c, yfar(j), x, z)).start())

        @pl.when(h == c)
        def _():
            wait_bytes(qx[k], r4.at[k])
            qb[k][v, 0] = qx[k][0] + qx[k][1]
            qb[k][v, 1] = qx[k][2] + qx[k][3]
            each(1, NY, lambda j: remote(qb[k].at[v], qb[k].at[v], s6.at[k], r6.at[k], dev(l, c, yy(j), x, z)).start())

    def gathered(k):
        wait_bytes(rp[k].at[pl.ds(0, NY - 1)], r5.at[k])

        @pl.when(h == c)
        def _():
            wait_bytes(qb[k].at[0], r6.at[k])

        @pl.when(h != c)
        def _():
            wait_bytes(qb[k], r6.at[k])

    def inchip_x():
        ex[x] = sum_z(zb[NB], NB)
        remote(ex.at[x], ex.at[x], s3.at[NC], r3.at[NC], dev(l, c, y, 1 - x, z)).start()

    def inchip_y():
        wait_bytes(ex.at[0], r3.at[NC])
        eb[y] = ex[0] + ex[1]
        each(1, NY, lambda j: remote(eb.at[y], eb.at[y], s5.at[NT], r5.at[NT], dev(l, c, yy(j), x, z)).start())

    def slab_of(k):
        xcopy[k].wait_recv()

        def step(b, total):
            at = pl.ds(pl.multiple_of(b * BLK, BLK), BLK)
            return total + dot3(xt[chunk[k], at], abh[at, :], abl[at, :])

        return lax.fori_loop(0, HALF // BLK, step, jnp.zeros((SIZES[k], 2 * COLS), F32))

    def spread_z(i):
        k = NB + i
        slab = slab_of(k)
        z2[i][z, c] = slab[:, :128]
        z2[i][z, 1 - c] = slab[:, 128:]
        each(1, NZ, lambda j: remote(z2[i].at[z], z2[i].at[z], s2.at[k + 1], r2.at[k + 1], dev(l, c, y, x, zz(j))).start())

    def spread_xy(i):
        k = NB + i
        w2[i][...] = sum_z(z2[i], k + 1)
        mine = qb2[i].at[c * NX * NY + w]

        def send(o):
            to = place(o)
            remote(w2[i], rp2[i].at[w], s3.at[k], r3.at[k], dev(1 - l, c, *to, z)).start()
            remote(w2[i].at[1 - c], mine, s4.at[k], r4.at[k], dev(l, 1 - c, *to, z)).start()

        each(0, NX * NY, send)
        each(0, here_last, lambda o: remote(w2[i].at[c], mine, s4.at[k], r4.at[k], dev(l, c, *place(o), z)).start())
        pltpu.make_async_copy(w2[i].at[c], mine, r4.at[k]).start()

    eacc[...] = jnp.zeros_like(eacc)
    ccopy[1].wait_recv()
    inchip(1, True)
    ccopy[0].wait_recv()
    inchip(0, False)
    scatter(NB, eacc[...])
    scatter(0, slab_of(0))
    sum_y(NB)
    sum_y(0)
    scatter(1, slab_of(1))
    inchip_x()
    sum_y(1)
    gather_x(0)
    scatter(2, slab_of(2))
    spread_z(0)
    spread_z(1)
    sum_y(2)
    inchip_y()
    gather_y(0)
    gather_x(1)

    fcopy.wait_recv()
    f_hi, f_lo = split(jnp.concatenate([ft[0], ft[1]], 1))
    f_both = jnp.concatenate([f_hi, f_lo], 0)

    def project(b, _):
        at = pl.ds(pl.multiple_of(b * 256, 256), 256)
        v_hi, v_lo = split(jnp.concatenate([st[1, :, at], xt[:, at]], 0))
        both = dot(f_both, v_hi)
        to = pl.ds(pl.multiple_of(b % 4 * 256, 256), 256)
        tt[b // 4, :, to] = both[:RANK] + both[RANK:] + dot(f_hi, v_lo)
        return 0

    lax.fori_loop(0, HALF // 256, project, 0)
    tcopy = remote(tt.at[1 - c], tr, ts, trs, cpeer)
    tcopy.start()

    spread_xy(0)
    spread_xy(1)
    gather(2)
    gather_y(1)

    tcopy.wait_recv()
    core_ref[...] = tt[c] + tr[...]
    wait_bytes(eb.at[pl.ds(0, NY - 1)], r5.at[NT])
    for q in range(2):
        at = pl.ds(pl.multiple_of(l * 256 + q * 128, 128), 128)
        gram_ref[:, at] = jnp.concatenate([eb[q * 2 + i] * scale for i in range(2)], 0)

    for k in range(NC):
        if k < NT:
            gathered(k)
        else:
            wait_bytes(rp[k] if k < NB else rp2[k - NB], r3.at[k])
            wait_bytes(qb[k] if k < NB else qb2[k - NB], r4.at[k])

    def all_places(pieces):
        total = pieces[0]
        for piece in pieces[1:]:
            total += piece
        return total

    for q in range(2):
        direct, turned = [], []
        for k in range(NB):
            for i in range(2):
                if k < NT:
                    direct.append(rp[k][q * 2 + i])
                    turned.append(qb[k][i, q])
                else:
                    direct.append(rp[k][q * 2 + i] + rp[k][NY + q * 2 + i])
                    turned.append(qb[k][q, i] + qb[k][q, 2 + i])
        for i in range(NS):
            direct.append(all_places([rp2[i][j, q] for j in range(NX * NY)]))
            turned.append(all_places([qb2[i][q * NX * NY + j] for j in range(NX * NY)]))
        at = pl.ds(pl.multiple_of((1 - l) * 256 + q * 128, 128), 128)
        gram_ref[:, at] = (jnp.concatenate(direct, 0) + jnp.concatenate(turned, 0).T) * scale

    for i in range(2):
        ccopy[i].wait_send()
    fcopy.wait_send()
    tcopy.wait_send()
    for k in range(NC):
        xcopy[k].wait_send()
    for k in range(NB + 1):
        wait_bytes(p1[k], s1.at[k])
        wait_bytes(zb[k].at[pl.ds(0, NZ - 1)], s2.at[k])
    for k in range(NB):
        pieces = px[k] if k < NT else rp[k]
        wait_bytes(pieces, s3.at[k])

        @pl.when(h == c)
        def _():
            wait_bytes(pieces.at[pl.ds(0, pieces.shape[0] - 1)], s4.at[k])

        @pl.when(h != c)
        def _():
            wait_bytes(pieces, s4.at[k])

        if k < NT:
            wait_bytes(rp[k].at[pl.ds(0, NY - 1)], s5.at[k])

            @pl.when(h == c)
            def _():
                wait_bytes(zb[k].at[pl.ds(0, 2 * (NY - 1))], s6.at[k])

    wait_bytes(ex.at[0], s3.at[NC])
    wait_bytes(eb.at[pl.ds(0, NY - 1)], s5.at[NT])
    for i in range(NS):
        k = NB + i
        wait_bytes(z2[i].at[pl.ds(0, NZ - 1)], s2.at[k + 1])
        wait_bytes(rp2[i], s3.at[k])
        wait_bytes(qb2[i].at[pl.ds(0, 2 * NX * NY - 1)], s4.at[k])


def write(gram_ref, core_ref, gram_out, core_out, sems):
    copies = [
        pltpu.make_async_copy(gram_ref, gram_out, sems.at[0]),
        pltpu.make_async_copy(core_ref, core_out, sems.at[1]),
    ]
    for copy in copies:
        copy.start()
    for copy in copies:
        copy.wait()


def local(snapshot, factor):
    fibres = snapshot.shape[0] * lax.axis_size("plane")
    dma = pltpu.SemaphoreType.DMA

    def vmem(*shape, dtype=F32):
        return pltpu.VMEM(shape, dtype)

    pieces = [n // 2 for n in BIG]
    with_e = pieces + [COLS // 2]
    outs = [((COLS, 4 * COLS), F32), ((RANK, PART), F32)]
    made = pl.pallas_call(
        functools.partial(kernel, 1.0 / fibres),
        out_shape=[jax.ShapeDtypeStruct(*o) for o in outs],
        in_specs=[pl.BlockSpec(memory_space=pl.ANY), pl.BlockSpec(memory_space=pltpu.VMEM)],
        out_specs=[pl.BlockSpec(memory_space=pltpu.VMEM)] * 2,
        scratch_shapes=[
            vmem(2, HALF, COLS),
            vmem(2, HALF, COLS),
            vmem(2, COLS, HALF),
            vmem(COLS, HALF),
            vmem(2, RANK, COLS),
            vmem(HALF, 2 * COLS, dtype=BF16),
            vmem(HALF, 2 * COLS, dtype=BF16),
            vmem(COLS, 2 * COLS),
            vmem(2, RANK, PART),
            vmem(RANK, PART),
        ]
        + [vmem(NY, n, 128) for n in with_e]
        + [vmem(NY - 1, n, 128) for n in with_e]
        + [vmem(NZ, n, 128) for n in with_e]
        + [vmem(n, 128) for n in pieces]
        + [vmem(NY, n, 128) for n in pieces[:NT]]
        + [vmem(NX * NY, n, 128) for n in pieces[NT:]]
        + [vmem(2, 2, n, 128) for n in pieces[:NT]]
        + [vmem(2, NX * 2, n, 128) for n in pieces[NT:]]
        + [vmem(NX, n, 128) for n in pieces[:NT]]
        + [vmem(2 * NX, n, 128) for n in pieces[:NT]]
        + [vmem(NX, COLS // 2, 128), vmem(NY, COLS // 2, 128)]
        + [vmem(NZ, 2, n, 128) for n in SMALL]
        + [vmem(2, n, 128) for n in SMALL]
        + [vmem(NX * NY, 2, n, 128) for n in SMALL]
        + [vmem(2 * NX * NY, n, 128) for n in SMALL]
        + [dma((2,)), dma((2,)), dma((2,)), dma, dma, dma((NC,)), dma((NC,))]
        + [dma((NB + 1,)), dma((NB + 1,)), dma((NC + 1,)), dma((NC + 1,))]
        + [dma((NC + 1,)), dma((NC + 1,)), dma((NC,)), dma((NC,))]
        + [dma((NT + 1,)), dma((NT + 1,)), dma((NT,)), dma((NT,)), dma, dma],
        compiler_params=pltpu.CompilerParams(
            collective_id=0, has_side_effects=True, vmem_limit_bytes=60 * 2**20
        ),
    )(snapshot, factor.T)
    return pl.pallas_call(
        write,
        out_shape=[jax.ShapeDtypeStruct(*o) for o in outs],
        in_specs=[pl.BlockSpec(memory_space=pltpu.VMEM)] * 2,
        out_specs=[pl.BlockSpec(memory_space=pl.ANY)] * 2,
        scratch_shapes=[dma((2,))],
    )(*made)


def solution(mesh):
    return jax.shard_map(
        local,
        mesh=mesh,
        in_specs=(P("plane", "span"), P("span", None)),
        out_specs=(P("span", None), P(None, ("plane", "span"))),
        check_vma=False,
    )
```
